32 devices in a mesh: seq: 8 (over y, x, core), fsdp: 4 (over z).
Axes of the slice: x: 2, y: 2, z: 4, core: 2. Of those that a mesh axis runs over, the one named last changes fastest.
Arguments:
- real_tokens: bfloat16 [4, 512, 3072], P('fsdp', 'seq'), may hold values from -6 to 6
- gen_hidden: bfloat16 [4, 512, 3072], P('fsdp', 'seq'), may hold values from -6 to 6
- modulation: float32 [4, 2, 3072], P('fsdp'), may hold values from -3 to 3
- norm_gain: float32 [3072], replicated, may hold values from 0.5 to 1.5
- proj_weight: bfloat16 [3, 3072, 2048], P(None, None, 'fsdp'), may hold values from -4 to 4
Outputs:
- grad_hidden: bfloat16 [4, 512, 3072], P('fsdp', 'seq')
The draws below stay inside these ranges and needn't reach their ends.
All inputs are finite; a program needn't handle non-finite values.
Results may differ from the reference program's by a relative error of at most 0.012.
The reference program's roundings to bfloat16 on the way (of `fake_tokens`, `normed` and `grad_out`) count: a program that leaves them out, or rounds other values in their place, can miss the bound.
Values may be sent and summed in bfloat16 or wider, within the bound.
A program may use at most 128 MiB of HBM per device.

```python
import jax
import jax.numpy as jnp
from jax import lax

D = 3072
HEADS = 16
HEAD_DIM = 128
LENGTH = 512
BATCH = 4


def draw_proj_weight(key, part):
    columns = HEADS * HEAD_DIM
    drawn = jax.random.normal(jax.random.fold_in(key, 11), (3, D, columns), jnp.float32) * D ** (-0.5)
    return jnp.clip(drawn, -4.0, 4.0).astype(jnp.bfloat16)


def levels(stream_key, dims, split, smallest, largest):
    loudness = 1.0
    for dim, blocks in split:
        heights = jax.random.uniform(jax.random.fold_in(jax.random.fold_in(stream_key, 6), dim), (blocks,), jnp.float32, smallest / len(split), largest / len(split))
        loudness = loudness * jnp.repeat(jnp.exp(heights), dims[dim] // blocks).reshape((-1,) + (1,) * (len(dims) - 1 - dim))
    return loudness


def bell_draw(key, extent, deviation, bound, cuts=(), kind=jnp.bfloat16):
    result = jax.random.normal(key, extent, jnp.float32) * deviation
    if len(cuts) > 0:
        result = levels(key, extent, cuts, -0.22, 0.18) * result
    return jnp.clip(result, min=-bound, max=bound).astype(kind)


def setup_inputs(seed: int = 0) -> dict:
    arg_keys = jax.random.split(jax.random.key(seed), 6)
    real_tokens = bell_draw(arg_keys[0], (BATCH, LENGTH, D), 1.0, 6.0, ((0, 4), (1, 8)))
    gen_hidden = bell_draw(arg_keys[1], (BATCH, LENGTH, D), 1.0, 6.0, ((0, 4), (1, 8)))
    modulation = bell_draw(arg_keys[2], (BATCH, 2, D), 0.5, 3.0, ((0, 4),), jnp.float32)
    norm_gain = jnp.clip(1.0 + 0.1 * jax.random.normal(arg_keys[3], (D,), jnp.float32), 0.5, 1.5)
    proj_weight = draw_proj_weight(jax.random.fold_in(arg_keys[5], 71), 0)
    return dict(real_tokens=real_tokens, gen_hidden=gen_hidden, modulation=modulation, norm_gain=norm_gain, proj_weight=proj_weight)


norm_eps = 1e-06
match_eps = 0.05
loss_weight = 4.0

def to_wide(values):
    return lax.optimization_barrier(values).astype(jnp.float32)

def normalize(tokens, norm_gain):
    values = to_wide(tokens)
    inverse = lax.rsqrt(lax.optimization_barrier(jnp.mean(values * values, axis=-1, keepdims=True)) + norm_eps)
    return ((values * inverse * norm_gain).astype(jnp.bfloat16), inverse)

def attend(queries, key_rows, value_rows):
    scores = jnp.einsum('qhd,khd->hqk', to_wide(queries), to_wide(key_rows)) * HEAD_DIM ** (-0.5)
    highest = lax.optimization_barrier(jnp.max(scores, axis=-1, keepdims=True))
    weights = jnp.exp(scores - highest)
    totals = lax.optimization_barrier(jnp.sum(weights, axis=-1, keepdims=True))
    mixed_values = jnp.einsum('hqk,khd->qhd', to_wide(weights.astype(jnp.bfloat16)), to_wide(value_rows))
    outputs = mixed_values / jnp.transpose(totals, (1, 0, 2))
    return (outputs, highest + jnp.log(totals))

def match_grad(fake_out, real_out):
    differ = fake_out - real_out
    return (loss_weight * differ / jnp.sqrt(differ * differ + match_eps * match_eps)).astype(jnp.bfloat16)

def row_delta(grad_out, fake_out):
    return lax.optimization_barrier(jnp.sum(to_wide(grad_out) * fake_out, axis=-1))

def backward_scores(queries, key_rows, value_rows, log_total, deltas, grad_out):
    scores = jnp.einsum('qhd,khd->hqk', to_wide(queries), to_wide(key_rows)) * HEAD_DIM ** (-0.5)
    probs = jnp.exp(scores - log_total)
    dprobs = jnp.einsum('qhd,khd->hqk', to_wide(grad_out), to_wide(value_rows))
    dscores = (probs * (dprobs - jnp.transpose(deltas)[:, :, None]) * HEAD_DIM ** (-0.5)).astype(jnp.bfloat16)
    return (probs.astype(jnp.bfloat16), dscores)

def one_sequence(real_row, hidden_row, modulation_row, norm_gain, proj_weight):
    seq_rows = real_row.shape[0]
    weight_wide = proj_weight.astype(jnp.float32)
    fake_tokens = (hidden_row.astype(jnp.float32) * (1.0 + modulation_row[0]) + modulation_row[1]).astype(jnp.bfloat16)
    real_normed, real_inverse = normalize(real_row, norm_gain)
    fake_normed, fake_inverse = normalize(fake_tokens, norm_gain)

    def project(normed):
        mapped = jnp.einsum('td,kdc->ktc', to_wide(normed), weight_wide).astype(jnp.bfloat16)
        return mapped.reshape(3, seq_rows, HEADS, HEAD_DIM)
    real_map = project(real_normed)
    fake_map = project(fake_normed)
    real_out, real_total = attend(real_map[0], real_map[1], real_map[2])
    fake_out, fake_total = attend(fake_map[0], fake_map[1], fake_map[2])
    grad_out = match_grad(fake_out, real_out)
    deltas = row_delta(grad_out, fake_out)
    prob_low, dscores = backward_scores(fake_map[0], fake_map[1], fake_map[2], fake_total, deltas, grad_out)
    grad_query = jnp.einsum('hqk,khd->qhd', to_wide(dscores), to_wide(fake_map[1]))
    grad_key = jnp.einsum('hqk,qhd->khd', to_wide(dscores), to_wide(fake_map[0]))
    grad_value = jnp.einsum('hqk,qhd->khd', to_wide(prob_low), to_wide(grad_out))
    all_grads = jnp.stack([grad_query, grad_key, grad_value]).astype(jnp.bfloat16)
    all_grads = all_grads.reshape(3, seq_rows, HEADS * HEAD_DIM)
    grad_normed = jnp.einsum('ktc,kdc->td', to_wide(all_grads), weight_wide)
    scaled = to_wide(fake_tokens) * fake_inverse
    grad_scaled = grad_normed * norm_gain
    grad_fake = fake_inverse * (grad_scaled - scaled * lax.optimization_barrier(jnp.mean(grad_scaled * scaled, axis=-1, keepdims=True)))
    return (grad_fake * (1.0 + modulation_row[0])).astype(jnp.bfloat16)

def reference(real_tokens, gen_hidden, modulation, norm_gain, proj_weight):

    def per_sequence(packed):
        return one_sequence(packed[0], packed[1], packed[2], norm_gain, proj_weight)
    return lax.map(per_sequence, (real_tokens, gen_hidden, modulation))
```

```python
import jax
import jax.numpy as jnp
from jax import lax
from jax.sharding import PartitionSpec as P

HEAD_DIM = 128


norm_eps = 1e-06
match_eps = 0.05
loss_weight = 4.0


def to_wide(values):
    return lax.optimization_barrier(values).astype(jnp.float32)


def normalize(tokens, norm_gain):
    values = to_wide(tokens)
    inverse = lax.rsqrt(jnp.mean(values * values, axis=-1, keepdims=True) + norm_eps)
    return ((values * inverse * norm_gain).astype(jnp.bfloat16), inverse)


def attend(queries, key_rows, value_rows):
    scores = jnp.einsum(
        "qhd,khd->hqk", queries, key_rows, preferred_element_type=jnp.float32
    ) * HEAD_DIM ** (-0.5)
    highest = jnp.max(scores, axis=-1, keepdims=True)
    weights = jnp.exp(scores - highest)
    totals = jnp.sum(weights, axis=-1, keepdims=True)
    mixed_values = jnp.einsum(
        "hqk,khd->qhd", weights.astype(jnp.bfloat16), value_rows, preferred_element_type=jnp.float32
    )
    outputs = mixed_values / jnp.transpose(totals, (1, 0, 2))
    return (outputs, highest + jnp.log(totals))


def match_grad(fake_out, real_out):
    differ = fake_out - real_out
    return (loss_weight * differ / jnp.sqrt(differ * differ + match_eps * match_eps)).astype(
        jnp.bfloat16
    )


def row_delta(grad_out, fake_out):
    return jnp.sum(to_wide(grad_out) * fake_out, axis=-1)


def backward_scores(queries, key_rows, value_rows, log_total, deltas, grad_out):
    scores = jnp.einsum(
        "qhd,khd->hqk", queries, key_rows, preferred_element_type=jnp.float32
    ) * HEAD_DIM ** (-0.5)
    probs = jnp.exp(scores - log_total)
    dprobs = jnp.einsum("qhd,khd->hqk", grad_out, value_rows, preferred_element_type=jnp.float32)
    dscores = (probs * (dprobs - jnp.transpose(deltas)[:, :, None]) * HEAD_DIM ** (-0.5)).astype(
        jnp.bfloat16
    )
    return (probs.astype(jnp.bfloat16), dscores)


def on_device(real_tokens, gen_hidden, modulation, norm_gain, proj_weight):
    tok_count = real_tokens.shape[1]
    fake_tokens = (
        gen_hidden[0].astype(jnp.float32) * (1.0 + modulation[0, 0]) + modulation[0, 1]
    ).astype(jnp.bfloat16)
    real_normed, real_inverse = normalize(real_tokens[0], norm_gain)
    fake_normed, fake_inverse = normalize(fake_tokens, norm_gain)
    both_normed = jnp.stack([real_normed, fake_normed])
    group, ranks = lax.axis_size("fsdp"), lax.axis_size("seq")
    owned = proj_weight.shape[2] // HEAD_DIM
    each = group * owned // ranks
    projected = jnp.einsum(
        "gstd,kdhc->ghkstc",
        lax.all_gather(both_normed, "fsdp", axis=0),
        proj_weight.reshape(proj_weight.shape[:2] + (owned, HEAD_DIM)),
        preferred_element_type=jnp.float32,
    ).astype(jnp.bfloat16)
    projected = projected.reshape(ranks, each, 3, 2, tok_count, HEAD_DIM)
    spread = lax.all_to_all(projected, "seq", split_axis=0, concat_axis=0)
    spread = jnp.transpose(spread, (2, 3, 0, 4, 1, 5)).reshape(
        3, 2, ranks * tok_count, each, HEAD_DIM
    )
    real_out, real_total = attend(spread[0, 0], spread[1, 0], spread[2, 0])
    fake_out, fake_total = attend(spread[0, 1], spread[1, 1], spread[2, 1])
    grad_out = match_grad(fake_out, real_out)
    deltas = row_delta(grad_out, fake_out)
    prob_low, dscores = backward_scores(
        spread[0, 1], spread[1, 1], spread[2, 1], fake_total, deltas, grad_out
    )
    grad_query = jnp.einsum(
        "hqk,khd->qhd", dscores, spread[1, 1], preferred_element_type=jnp.float32
    )
    grad_key = jnp.einsum("hqk,qhd->khd", dscores, spread[0, 1], preferred_element_type=jnp.float32)
    grad_value = jnp.einsum("hqk,qhd->khd", prob_low, grad_out, preferred_element_type=jnp.float32)
    local_grads = jnp.stack([grad_query, grad_key, grad_value]).astype(jnp.bfloat16)
    local_grads = local_grads.reshape(3, ranks, tok_count, each, HEAD_DIM)
    all_grads = lax.all_to_all(
        jnp.transpose(local_grads, (1, 3, 0, 2, 4)), "seq", split_axis=0, concat_axis=0
    ).reshape(group, owned, 3, tok_count, HEAD_DIM)
    owner_grads = jnp.transpose(all_grads, (2, 0, 3, 1, 4)).reshape(3, group * tok_count, -1)
    grad_normed = lax.psum_scatter(
        jnp.einsum(
            "ktc,kdc->td", owner_grads, proj_weight, preferred_element_type=jnp.float32
        ).astype(jnp.bfloat16),
        "fsdp",
        scatter_dimension=0,
        tiled=True,
    ).astype(jnp.float32)
    scaled = to_wide(fake_tokens) * fake_inverse
    grad_scaled = grad_normed * norm_gain
    grad_fake = fake_inverse * (
        grad_scaled - scaled * jnp.mean(grad_scaled * scaled, axis=-1, keepdims=True)
    )
    grad_hidden = (grad_fake * (1.0 + modulation[0, 0])).astype(jnp.bfloat16)
    return grad_hidden[None]


def solution(mesh):
    placed = (
        P("fsdp", "seq", None),
        P("fsdp", "seq", None),
        P("fsdp", None, None),
        P(),
        P(None, None, "fsdp"),
    )
    return jax.shard_map(
        on_device, mesh=mesh, in_specs=placed, out_specs=P("fsdp", "seq", None), check_vma=False
    )
```

```python
import functools

import jax
import jax.numpy as jnp
from jax import lax
from jax.experimental import pallas as pl
from jax.experimental.pallas import tpu as pltpu
from jax.sharding import PartitionSpec as P

HEAD_DIM = 128
norm_eps = 1e-06
match_eps = 0.05
loss_weight = 4.0
MESH = pl.DeviceIdType.MESH
NT = (((1,), (1,)), ((), ()))
TN = (((0,), (0,)), ((), ()))


def mm(a, b, dims=(((1,), (0,)), ((), ()))):
    return lax.dot_general(a, b, dims, preferred_element_type=jnp.float32)


def kernel(
    group, ranks, owned, each,
    real_ref, hidden_ref, mod_ref, gain_ref, weight_ref, out_ref,
    weight, gath, tokens, inverse, stage, qkv, grad_key, grad_value, gstage, grecv,
    partial, sums, arrived,
    weight_sem, ag_send, ag_recv, fw_send, fw_recv, bw_send, bw_recv, rs_send, rs_recv,
):
    me, plane = lax.axis_index("seq"), lax.axis_index("fsdp")
    count, width = real_ref.shape[1], real_ref.shape[2]
    length = ranks * count
    pairs = group * owned
    scale = HEAD_DIM ** (-0.5)
    columns = owned * HEAD_DIM

    barrier = pltpu.get_barrier_semaphore()
    for other in range(ranks):
        @pl.when(other != me)
        def _():
            pl.semaphore_signal(barrier, inc=1, device_id={"seq": other}, device_id_type=MESH)

    @pl.when(plane > 0)
    def _():
        pl.semaphore_signal(barrier, inc=1, device_id={"fsdp": plane - 1}, device_id_type=MESH)

    @pl.when(plane < group - 1)
    def _():
        pl.semaphore_signal(barrier, inc=1, device_id={"fsdp": plane + 1}, device_id_type=MESH)

    loads = [pltpu.make_async_copy(weight_ref.at[k], weight.at[k], weight_sem.at[k]) for k in range(3)]
    for load in loads:
        load.start()

    rows_each = 16
    scale_row = 1.0 + mod_ref[0, 0:1, :]
    shift_row = mod_ref[0, 1:2, :]

    def normed_rows(values):
        inv = lax.rsqrt(jnp.mean(values * values, axis=-1, keepdims=True) + norm_eps)
        return (values * inv * gain_ref[...]).astype(jnp.bfloat16), inv

    @pl.loop(0, count // rows_each)
    def _(i):
        rows = pl.ds(pl.multiple_of(i * rows_each, rows_each), rows_each)
        gath[plane, 0, rows, :] = normed_rows(real_ref[0, rows, :].astype(jnp.float32))[0]

    peers = ranks - 1 + (plane > 0).astype(jnp.int32) + (plane < group - 1).astype(jnp.int32)
    pl.semaphore_wait(barrier, peers)

    toward = (plane + 1, plane - 1)
    has_next = (plane < group - 1, plane > 0)
    has_prev = (plane > 0, plane < group - 1)

    def handed(way, hop, stream, block):
        return pltpu.make_async_remote_copy(
            src_ref=gath.at[block, stream], dst_ref=gath.at[block, stream],
            send_sem=ag_send.at[way, hop, stream], recv_sem=ag_recv.at[way, hop, stream],
            device_id={"fsdp": toward[way]}, device_id_type=MESH,
        )

    def sent_block(way, hop):
        return plane - hop if way == 0 else plane + hop

    def got_block(way, hop):
        return plane - 1 - hop if way == 0 else plane + 1 + hop

    def inside(block):
        return (block >= 0) & (block < group)

    def give(way, hop, stream):
        @pl.when(has_next[way] & inside(sent_block(way, hop)))
        def _():
            handed(way, hop, stream, sent_block(way, hop)).start()

    def forward_copy(stream, pair):
        return pltpu.make_async_remote_copy(
            src_ref=stage.at[stream, pair], dst_ref=qkv.at[lax.rem(pair, each), stream, :, me],
            send_sem=fw_send.at[stream, pair], recv_sem=fw_recv.at[stream, lax.rem(pair, each), me],
            device_id={"seq": lax.div(pair, each)}, device_id_type=MESH,
        )

    wide = min(256, columns)

    def project(block, stream):
        @pl.loop(0, 3 * (columns // wide))
        def _(i):
            k, tile = lax.div(i, columns // wide), lax.rem(i, columns // wide)
            cols = pl.ds(pl.multiple_of(tile * wide, wide), wide)
            done = mm(gath[block, stream], weight[k, :, cols]).astype(jnp.bfloat16)
            for h in range(wide // HEAD_DIM):
                pair = block * owned + tile * (wide // HEAD_DIM) + h
                stage[stream, pair, k] = done[:, h * HEAD_DIM : (h + 1) * HEAD_DIM]

        for j in range(owned):
            pair = block * owned + j

            @pl.when(lax.div(pair, each) != me)
            def _():
                forward_copy(stream, pair).start()

            @pl.when(lax.div(pair, each) == me)
            def _():
                e = lax.rem(pair, each)
                pltpu.make_async_copy(
                    stage.at[stream, pair], qkv.at[e, stream, :, me], fw_recv.at[stream, e, me]
                ).start()

    for way in range(2):
        give(way, 0, 0)

    @pl.loop(0, count // rows_each)
    def _(i):
        rows = pl.ds(pl.multiple_of(i * rows_each, rows_each), rows_each)
        fake = (hidden_ref[0, rows, :].astype(jnp.float32) * scale_row + shift_row).astype(jnp.bfloat16)
        tokens[rows, :] = fake
        normed, inv = normed_rows(fake.astype(jnp.float32))
        gath[plane, 1, rows, :] = normed
        inverse[rows, :] = jnp.broadcast_to(inv, (rows_each, HEAD_DIM))

    for way in range(2):
        give(way, 0, 1)
    for load in loads:
        load.wait()

    @pl.loop(0, 2)
    def _(stream):
        project(plane, stream)

    @pl.loop(0, 2 * (group - 1))
    def _(step):
        hop, stream = lax.div(step, 2), lax.rem(step, 2)
        for way in range(2):
            @pl.when(inside(got_block(way, hop)))
            def _():
                handed(way, hop, stream, got_block(way, hop)).wait_recv()

                @pl.when(hop + 1 < group - 1)
                def _():
                    give(way, hop + 1, stream)

        for way in range(2):
            @pl.when(inside(got_block(way, hop)))
            def _():
                project(got_block(way, hop), stream)

    block_rows = 256 if length % 256 == 0 else length
    block_parts = block_rows // count

    def flat(values):
        return values.reshape(-1, HEAD_DIM)

    def back_copy(e, other):
        return pltpu.make_async_remote_copy(
            src_ref=gstage.at[e, :, other], dst_ref=grecv.at[me * each + e],
            send_sem=bw_send.at[e, other], recv_sem=bw_recv.at[me * each + e],
            device_id={"seq": other}, device_id_type=MESH,
        )

    @pl.loop(0, each)
    def _(e):
        for stream in range(2):
            @pl.loop(0, ranks)
            def _(source):
                pltpu.make_async_copy(
                    stage.at[stream, 0], qkv.at[e, stream, :, source], fw_recv.at[stream, e, source]
                ).wait()

        grad_key[...] = jnp.zeros_like(grad_key)
        grad_value[...] = jnp.zeros_like(grad_value)

        @pl.loop(0, length // block_rows)
        def _(b):
            parts = pl.ds(b * block_parts, block_parts)

            def attend(stream):
                queries = flat(qkv[e, stream, 0, parts])
                scores = mm(queries, flat(qkv[e, stream, 1]), NT) * scale
                weights = jnp.exp(scores - jnp.max(scores, axis=-1, keepdims=True))
                share = 1.0 / jnp.sum(weights, axis=-1, keepdims=True)
                mixed = mm(weights.astype(jnp.bfloat16), flat(qkv[e, stream, 2])) * share
                return queries, weights, share, mixed

            real_out = attend(0)[3]
            queries, weights, share, fake_out = attend(1)
            differ = fake_out - real_out
            grad_out = (loss_weight * differ * lax.rsqrt(differ * differ + match_eps * match_eps)).astype(jnp.bfloat16)
            deltas = jnp.sum(grad_out.astype(jnp.float32) * fake_out, axis=-1, keepdims=True)
            probs = weights * share
            dprobs = mm(grad_out, flat(qkv[e, 1, 2]), NT)
            dscores = (probs * (dprobs - deltas) * scale).astype(jnp.bfloat16)
            grad_query = mm(dscores, flat(qkv[e, 1, 1])).astype(jnp.bfloat16)
            gstage[e, 0, parts] = grad_query.reshape(block_parts, count, HEAD_DIM)
            grad_key[...] += mm(dscores, queries, TN)
            grad_value[...] += mm(probs.astype(jnp.bfloat16), grad_out, TN)

        gstage[e, 1] = grad_key[...].astype(jnp.bfloat16).reshape(ranks, count, HEAD_DIM)
        gstage[e, 2] = grad_value[...].astype(jnp.bfloat16).reshape(ranks, count, HEAD_DIM)

        @pl.loop(0, ranks)
        def _(other):
            @pl.when(other != me)
            def _():
                back_copy(e, other).start()

            @pl.when(other == me)
            def _():
                pltpu.make_async_copy(
                    gstage.at[e, :, me], grecv.at[me * each + e], bw_recv.at[me * each + e]
                ).start()

    deep = 512 if width % 512 == 0 else width

    def grad_rows(block):
        for j in range(owned):
            pair = block * owned + j
            pltpu.make_async_copy(gstage.at[0, :, 0], grecv.at[pair], bw_recv.at[pair]).wait()

        @pl.loop(0, width // deep)
        def _(i):
            at = pl.ds(pl.multiple_of(i * deep, deep), deep)
            total = None
            for k in range(3):
                rows = jnp.concatenate([grecv[block * owned + j, k] for j in range(owned)], axis=1)
                term = mm(rows, weight[k, at, :], NT)
                total = term if total is None else total + term
            partial[:, at] = total

    def sum_copy(way, block):
        return pltpu.make_async_remote_copy(
            src_ref=sums.at[block], dst_ref=arrived.at[way, block],
            send_sem=rs_send.at[way, block], recv_sem=rs_recv.at[way, block],
            device_id={"fsdp": toward[way]}, device_id_type=MESH,
        )

    def add_arrived(way, block):
        @pl.when(has_prev[way])
        def _():
            sum_copy(way, block).wait_recv()
            partial[...] += arrived[way, block].astype(jnp.float32)

    @pl.loop(0, group - 1)
    def _(step):
        for way in range(2):
            block = group - 1 - step if way == 0 else step

            @pl.when((block > plane) if way == 0 else (block < plane))
            def _():
                grad_rows(block)
                add_arrived(way, block)
                sums[block] = partial[...].astype(jnp.bfloat16)
                sum_copy(way, block).start()

    grad_rows(plane)
    for way in range(2):
        add_arrived(way, plane)

    @pl.loop(0, count // rows_each)
    def _(i):
        rows = pl.ds(pl.multiple_of(i * rows_each, rows_each), rows_each)
        inv = inverse[rows, 0:1]
        scaled = tokens[rows, :].astype(jnp.float32) * inv
        grad_scaled = partial[rows, :] * gain_ref[...]
        mean = jnp.mean(grad_scaled * scaled, axis=-1, keepdims=True)
        out_ref[0, rows, :] = (inv * (grad_scaled - scaled * mean) * scale_row).astype(jnp.bfloat16)

    for way in range(2):
        @pl.loop(0, group - 1)
        def _(hop):
            @pl.when(has_next[way] & inside(sent_block(way, hop)))
            def _():
                for stream in range(2):
                    handed(way, hop, stream, sent_block(way, hop)).wait_send()

        @pl.loop(0, group)
        def _(block):
            @pl.when((block > plane) if way == 0 else (block < plane))
            def _():
                sum_copy(way, block).wait_send()

    @pl.loop(0, pairs)
    def _(pair):
        @pl.when(lax.div(pair, each) != me)
        def _():
            for stream in range(2):
                forward_copy(stream, pair).wait_send()

    @pl.loop(0, ranks)
    def _(other):
        @pl.when(other != me)
        def _():
            for e in range(each):
                back_copy(e, other).wait_send()


def on_device(group, ranks, real_tokens, gen_hidden, modulation, norm_gain, proj_weight):
    _, count, width = real_tokens.shape
    columns = proj_weight.shape[2]
    owned = columns // HEAD_DIM
    pairs = group * owned
    each = pairs // ranks
    low, full = jnp.bfloat16, jnp.float32
    dma = pltpu.SemaphoreType.DMA
    vmem = pl.BlockSpec(memory_space=pltpu.VMEM)
    return pl.pallas_call(
        functools.partial(kernel, group, ranks, owned, each),
        out_shape=jax.ShapeDtypeStruct(real_tokens.shape, low),
        in_specs=[vmem] * 4 + [pl.BlockSpec(memory_space=pl.ANY)],
        out_specs=vmem,
        scratch_shapes=[
            pltpu.VMEM((3, width, columns), low),
            pltpu.VMEM((group, 2, count, width), low),
            pltpu.VMEM((count, width), low),
            pltpu.VMEM((count, HEAD_DIM), full),
            pltpu.VMEM((2, pairs, 3, count, HEAD_DIM), low),
            pltpu.VMEM((each, 2, 3, ranks, count, HEAD_DIM), low),
            pltpu.VMEM((ranks * count, HEAD_DIM), full),
            pltpu.VMEM((ranks * count, HEAD_DIM), full),
            pltpu.VMEM((each, 3, ranks, count, HEAD_DIM), low),
            pltpu.VMEM((pairs, 3, count, HEAD_DIM), low),
            pltpu.VMEM((count, width), full),
            pltpu.VMEM((group, count, width), low),
            pltpu.VMEM((2, group, count, width), low),
            dma((3,)),
            dma((2, group - 1, 2)),
            dma((2, group - 1, 2)),
            dma((2, pairs)),
            dma((2, each, ranks)),
            dma((each, ranks)),
            dma((pairs,)),
            dma((2, group)),
            dma((2, group)),
        ],
        compiler_params=pltpu.CompilerParams(
            collective_id=0, has_side_effects=True, vmem_limit_bytes=56 * 1024 * 1024
        ),
    )(real_tokens, gen_hidden, modulation, norm_gain.reshape(1, width), proj_weight)


def solution(mesh):
    placed = (
        P("fsdp", "seq", None),
        P("fsdp", "seq", None),
        P("fsdp", None, None),
        P(),
        P(None, None, "fsdp"),
    )
    return jax.shard_map(
        functools.partial(on_device, mesh.shape["fsdp"], mesh.shape["seq"]),
        mesh=mesh, in_specs=placed, out_specs=P("fsdp", "seq", None), check_vma=False,
    )
```

```python
import functools

import jax
import jax.numpy as jnp
from jax import lax
from jax.experimental import pallas as pl
from jax.experimental.pallas import tpu as pltpu
from jax.sharding import PartitionSpec as P

HEAD_DIM = 128
norm_eps = 1e-06
match_eps = 0.05
loss_weight = 4.0
MESH = pl.DeviceIdType.MESH
NT = (((1,), (1,)), ((), ()))
TN = (((0,), (0,)), ((), ()))


def mm(a, b, dims=(((1,), (0,)), ((), ()))):
    return lax.dot_general(a, b, dims, preferred_element_type=jnp.float32)


def kernel(
    group, ranks, owned, each,
    real_ref, hidden_ref, mod_ref, gain_ref, weight_ref, out_ref,
    weight, gath, tokens, inverse, stage, qkv, grad_key, grad_value, gstage, grecv,
    partial, sums, arrived,
    weight_sem, ag_send, ag_recv, fw_send, fw_recv, bw_send, bw_recv, rs_send, rs_recv,
):
    me, plane = lax.axis_index("seq"), lax.axis_index("fsdp")
    count, width = real_ref.shape[1], real_ref.shape[2]
    length = ranks * count
    pairs = group * owned
    scale = HEAD_DIM ** (-0.5)
    columns = owned * HEAD_DIM

    barrier = pltpu.get_barrier_semaphore()
    for other in range(ranks):
        @pl.when(other != me)
        def _():
            pl.semaphore_signal(barrier, inc=1, device_id={"seq": other}, device_id_type=MESH)

    @pl.when(plane > 0)
    def _():
        pl.semaphore_signal(barrier, inc=1, device_id={"fsdp": plane - 1}, device_id_type=MESH)

    @pl.when(plane < group - 1)
    def _():
        pl.semaphore_signal(barrier, inc=1, device_id={"fsdp": plane + 1}, device_id_type=MESH)

    loads = [pltpu.make_async_copy(weight_ref.at[k], weight.at[k], weight_sem.at[k]) for k in range(3)]
    for load in loads:
        load.start()

    rows_each = 16
    scale_row = 1.0 + mod_ref[0, 0:1, :]
    shift_row = mod_ref[0, 1:2, :]

    def normed_rows(values):
        inv = lax.rsqrt(jnp.mean(values * values, axis=-1, keepdims=True) + norm_eps)
        return (values * inv * gain_ref[...]).astype(jnp.bfloat16), inv

    @pl.loop(0, count // rows_each)
    def _(i):
        rows = pl.ds(pl.multiple_of(i * rows_each, rows_each), rows_each)
        gath[plane, 0, rows, :] = normed_rows(real_ref[0, rows, :].astype(jnp.float32))[0]

    peers = ranks - 1 + (plane > 0).astype(jnp.int32) + (plane < group - 1).astype(jnp.int32)
    pl.semaphore_wait(barrier, peers)

    toward = (plane + 1, plane - 1)
    has_next = (plane < group - 1, plane > 0)

    def handed(way, hop, stream, block):
        return pltpu.make_async_remote_copy(
            src_ref=gath.at[block, stream], dst_ref=gath.at[block, stream],
            send_sem=ag_send.at[way, hop, stream], recv_sem=ag_recv.at[way, hop, stream],
            device_id={"fsdp": toward[way]}, device_id_type=MESH,
        )

    def sent_block(way, hop):
        return plane - hop if way == 0 else plane + hop

    def got_block(way, hop):
        return plane - 1 - hop if way == 0 else plane + 1 + hop

    def inside(block):
        return (block >= 0) & (block < group)

    def give(way, hop, stream):
        @pl.when(has_next[way] & inside(sent_block(way, hop)))
        def _():
            handed(way, hop, stream, sent_block(way, hop)).start()

    def forward_copy(stream, pair):
        return pltpu.make_async_remote_copy(
            src_ref=stage.at[stream, pair], dst_ref=qkv.at[lax.rem(pair, each), stream, :, me],
            send_sem=fw_send.at[stream, pair], recv_sem=fw_recv.at[stream, lax.rem(pair, each), me],
            device_id={"seq": lax.div(pair, each)}, device_id_type=MESH,
        )

    wide = min(256, columns)

    def project(block, stream):
        @pl.loop(0, 3 * (columns // wide))
        def _(i):
            k, tile = lax.div(i, columns // wide), lax.rem(i, columns // wide)
            cols = pl.ds(pl.multiple_of(tile * wide, wide), wide)
            done = mm(gath[block, stream], weight[k, :, cols]).astype(jnp.bfloat16)
            for h in range(wide // HEAD_DIM):
                pair = (tile * (wide // HEAD_DIM) + h) * group + block
                stage[stream, pair, k] = done[:, h * HEAD_DIM : (h + 1) * HEAD_DIM]

        for j in range(owned):
            pair = j * group + block

            @pl.when(lax.div(pair, each) != me)
            def _():
                forward_copy(stream, pair).start()

            @pl.when(lax.div(pair, each) == me)
            def _():
                e = lax.rem(pair, each)
                pltpu.make_async_copy(
                    stage.at[stream, pair], qkv.at[e, stream, :, me], fw_recv.at[stream, e, me]
                ).start()

    for way in range(2):
        give(way, 0, 0)

    @pl.loop(0, count // rows_each)
    def _(i):
        rows = pl.ds(pl.multiple_of(i * rows_each, rows_each), rows_each)
        fake = (hidden_ref[0, rows, :].astype(jnp.float32) * scale_row + shift_row).astype(jnp.bfloat16)
        tokens[rows, :] = fake
        normed, inv = normed_rows(fake.astype(jnp.float32))
        gath[plane, 1, rows, :] = normed
        inverse[rows, :] = jnp.broadcast_to(inv, (rows_each, HEAD_DIM))

    for way in range(2):
        give(way, 0, 1)
    for load in loads:
        load.wait()

    @pl.loop(0, 2)
    def _(stream):
        project(plane, stream)

    @pl.loop(0, 2 * (group - 1))
    def _(step):
        hop, stream = lax.div(step, 2), lax.rem(step, 2)
        for way in range(2):
            @pl.when(inside(got_block(way, hop)))
            def _():
                handed(way, hop, stream, got_block(way, hop)).wait_recv()

                @pl.when(hop + 1 < group - 1)
                def _():
                    give(way, hop + 1, stream)

        for way in range(2):
            @pl.when(inside(got_block(way, hop)))
            def _():
                project(got_block(way, hop), stream)

    block_rows = 256 if length % 256 == 0 else length
    block_parts = block_rows // count

    def flat(values):
        return values.reshape(-1, HEAD_DIM)

    def back_copy(e, other):
        return pltpu.make_async_remote_copy(
            src_ref=gstage.at[e, :, other], dst_ref=grecv.at[me * each + e],
            send_sem=bw_send.at[e, other], recv_sem=bw_recv.at[me * each + e],
            device_id={"seq": other}, device_id_type=MESH,
        )

    @pl.loop(0, each)
    def _(e):
        for stream in range(2):
            @pl.loop(0, ranks)
            def _(source):
                pltpu.make_async_copy(
                    stage.at[stream, 0], qkv.at[e, stream, :, source], fw_recv.at[stream, e, source]
                ).wait()

        grad_key[...] = jnp.zeros_like(grad_key)
        grad_value[...] = jnp.zeros_like(grad_value)

        @pl.loop(0, length // block_rows)
        def _(b):
            parts = pl.ds(b * block_parts, block_parts)

            def attend(stream):
                queries = flat(qkv[e, stream, 0, parts])
                scores = mm(queries, flat(qkv[e, stream, 1]), NT) * scale
                weights = jnp.exp(scores - jnp.max(scores, axis=-1, keepdims=True))
                share = 1.0 / jnp.sum(weights, axis=-1, keepdims=True)
                mixed = mm(weights.astype(jnp.bfloat16), flat(qkv[e, stream, 2])) * share
                return queries, weights, share, mixed

            real_out = attend(0)[3]
            queries, weights, share, fake_out = attend(1)
            differ = fake_out - real_out
            grad_out = (loss_weight * differ * lax.rsqrt(differ * differ + match_eps * match_eps)).astype(jnp.bfloat16)
            deltas = jnp.sum(grad_out.astype(jnp.float32) * fake_out, axis=-1, keepdims=True)
            probs = weights * share
            dprobs = mm(grad_out, flat(qkv[e, 1, 2]), NT)
            dscores = (probs * (dprobs - deltas) * scale).astype(jnp.bfloat16)
            grad_query = mm(dscores, flat(qkv[e, 1, 1])).astype(jnp.bfloat16)
            gstage[e, 0, parts] = grad_query.reshape(block_parts, count, HEAD_DIM)
            grad_key[...] += mm(dscores, queries, TN)
            grad_value[...] += mm(probs.astype(jnp.bfloat16), grad_out, TN)

        gstage[e, 1] = grad_key[...].astype(jnp.bfloat16).reshape(ranks, count, HEAD_DIM)
        gstage[e, 2] = grad_value[...].astype(jnp.bfloat16).reshape(ranks, count, HEAD_DIM)

        @pl.loop(1, ranks)
        def _(away):
            back_copy(e, lax.rem(me + away, ranks)).start()

        pltpu.make_async_copy(
            gstage.at[e, :, me], grecv.at[me * each + e], bw_recv.at[me * each + e]
        ).start()

    deep = 512 if width % 512 == 0 else width

    def grad_rows(block):
        for j in range(owned):
            pair = j * group + block
            pltpu.make_async_copy(gstage.at[0, :, 0], grecv.at[pair], bw_recv.at[pair]).wait()

        @pl.loop(0, width // deep)
        def _(i):
            at = pl.ds(pl.multiple_of(i * deep, deep), deep)
            total = None
            for k in range(3):
                rows = jnp.concatenate([grecv[j * group + block, k] for j in range(owned)], axis=1)
                term = mm(rows, weight[k, at, :], NT)
                total = term if total is None else total + term
            partial[:, at] = total

    def sum_copy(way, block):
        return pltpu.make_async_remote_copy(
            src_ref=sums.at[block], dst_ref=arrived.at[way, block],
            send_sem=rs_send.at[way, block], recv_sem=rs_recv.at[way, block],
            device_id={"fsdp": jnp.where(way == 0, plane + 1, plane - 1)}, device_id_type=MESH,
        )

    def add_arrived(way, block):
        @pl.when(((way == 0) & (plane > 0)) | ((way == 1) & (plane < group - 1)))
        def _():
            sum_copy(way, block).wait_recv()
            partial[...] += arrived[way, block].astype(jnp.float32)

    near = (2 * plane > group - 1).astype(jnp.int32)

    @pl.loop(0, 2 * (group - 1))
    def _(turn):
        step, way = lax.div(turn, 2), lax.rem(near + turn, 2)
        block = jnp.where(way == 0, group - 1 - step, step)

        @pl.when(((way == 0) & (block > plane)) | ((way == 1) & (block < plane)))
        def _():
            grad_rows(block)
            add_arrived(way, block)
            sums[block] = partial[...].astype(jnp.bfloat16)
            sum_copy(way, block).start()

    grad_rows(plane)

    @pl.loop(0, 2)
    def _(turn):
        add_arrived(lax.rem(near + turn, 2), plane)

    @pl.loop(0, count // rows_each)
    def _(i):
        rows = pl.ds(pl.multiple_of(i * rows_each, rows_each), rows_each)
        inv = inverse[rows, 0:1]
        scaled = tokens[rows, :].astype(jnp.float32) * inv
        grad_scaled = partial[rows, :] * gain_ref[...]
        mean = jnp.mean(grad_scaled * scaled, axis=-1, keepdims=True)
        out_ref[0, rows, :] = (inv * (grad_scaled - scaled * mean) * scale_row).astype(jnp.bfloat16)

    for way in range(2):
        @pl.loop(0, group - 1)
        def _(hop):
            @pl.when(has_next[way] & inside(sent_block(way, hop)))
            def _():
                for stream in range(2):
                    handed(way, hop, stream, sent_block(way, hop)).wait_send()

        @pl.loop(0, group)
        def _(block):
            @pl.when((block > plane) if way == 0 else (block < plane))
            def _():
                sum_copy(way, block).wait_send()

    @pl.loop(0, pairs)
    def _(pair):
        @pl.when(lax.div(pair, each) != me)
        def _():
            for stream in range(2):
                forward_copy(stream, pair).wait_send()

    @pl.loop(0, ranks)
    def _(other):
        @pl.when(other != me)
        def _():
            for e in range(each):
                back_copy(e, other).wait_send()


def on_device(group, ranks, real_tokens, gen_hidden, modulation, norm_gain, proj_weight):
    _, count, width = real_tokens.shape
    columns = proj_weight.shape[2]
    owned = columns // HEAD_DIM
    pairs = group * owned
    each = pairs // ranks
    low, full = jnp.bfloat16, jnp.float32
    dma = pltpu.SemaphoreType.DMA
    vmem = pl.BlockSpec(memory_space=pltpu.VMEM)
    return pl.pallas_call(
        functools.partial(kernel, group, ranks, owned, each),
        out_shape=jax.ShapeDtypeStruct(real_tokens.shape, low),
        in_specs=[vmem] * 4 + [pl.BlockSpec(memory_space=pl.ANY)],
        out_specs=vmem,
        scratch_shapes=[
            pltpu.VMEM((3, width, columns), low),
            pltpu.VMEM((group, 2, count, width), low),
            pltpu.VMEM((count, width), low),
            pltpu.VMEM((count, HEAD_DIM), full),
            pltpu.VMEM((2, pairs, 3, count, HEAD_DIM), low),
            pltpu.VMEM((each, 2, 3, ranks, count, HEAD_DIM), low),
            pltpu.VMEM((ranks * count, HEAD_DIM), full),
            pltpu.VMEM((ranks * count, HEAD_DIM), full),
            pltpu.VMEM((each, 3, ranks, count, HEAD_DIM), low),
            pltpu.VMEM((pairs, 3, count, HEAD_DIM), low),
            pltpu.VMEM((count, width), full),
            pltpu.VMEM((group, count, width), low),
            pltpu.VMEM((2, group, count, width), low),
            dma((3,)),
            dma((2, group - 1, 2)),
            dma((2, group - 1, 2)),
            dma((2, pairs)),
            dma((2, each, ranks)),
            dma((each, ranks)),
            dma((pairs,)),
            dma((2, group)),
            dma((2, group)),
        ],
        compiler_params=pltpu.CompilerParams(
            collective_id=0, has_side_effects=True, vmem_limit_bytes=56 * 1024 * 1024
        ),
    )(real_tokens, gen_hidden, modulation, norm_gain.reshape(1, width), proj_weight)


def solution(mesh):
    placed = (
        P("fsdp", "seq", None),
        P("fsdp", "seq", None),
        P("fsdp", None, None),
        P(),
        P(None, None, "fsdp"),
    )
    return jax.shard_map(
        functools.partial(on_device, mesh.shape["fsdp"], mesh.shape["seq"]),
        mesh=mesh, in_specs=placed, out_specs=P("fsdp", "seq", None), check_vma=False,
    )
```
